512 devices in a mesh: gx: 8 (over z_hi, y), gy: 8 (over x, core), gz: 8 (over z_lo).
Axes of the slice: x: 4, y: 4, z: 16 (z_hi: 2, z_lo: 8; z = z_hi * 8 + z_lo), core: 2. Of those that a mesh axis runs over, the one named last changes fastest.
Arguments:
- tokens: bfloat16 [2048, 6144], P('gy', ('gz', 'gx')), may hold values from -6 to 6
- up_weight: bfloat16 [6144, 24576], P(('gz', 'gy'), 'gx'), may hold values from -0.078125 to 0.078125
- down_weight: bfloat16 [24576, 6144], P('gx', ('gz', 'gy')), may hold values from -0.0390625 to 0.0390625
- grad_output: bfloat16 [2048, 6144], P('gy', ('gz', 'gx')), may hold values from -6 to 6
Outputs:
- output: bfloat16 [2048, 6144], P('gy', ('gz', 'gx'))
- grad_tokens: bfloat16 [2048, 6144], P('gy', ('gz', 'gx'))
The draws below stay inside these ranges and needn't reach their ends.
All inputs are finite; a program needn't handle non-finite values.
Results may differ from the reference program's by a relative error of at most 0.027.
Values may be sent and summed in bfloat16 or wider, within the bound.
No kernel may reach another device: no remote copies, remote signals or barrier semaphores. Data moves between devices by JAX's collectives and lax.ppermute only.
A program may use at most 64 MiB of HBM per device.

```python
import math
import jax
import jax.numpy as jnp
from jax import lax

D = 6144
FF = 24576
TOKENS = 2048
N_GX = 8
N_GZ = 8


def steps_of(rng, extent, cuts, least, high):
    level = 1.0
    for position, parts in cuts:
        heights = jax.random.uniform(jax.random.fold_in(jax.random.fold_in(rng, 6), position), (parts,), jnp.float32, least / len(cuts), high / len(cuts))
        level = level * jnp.repeat(jnp.exp(heights), extent[position] // parts).reshape((-1,) + (1,) * (len(extent) - 1 - position))
    return level


def gaussian(rng, dims, width, most, cuts=(), held_as=jnp.bfloat16):
    array = width * jax.random.normal(rng, dims, jnp.float32)
    if cuts:
        array = array * steps_of(rng, dims, cuts, -0.22, 0.18)
    return jnp.clip(array, -most, most).astype(held_as)


def setup_inputs(seed: int = 0) -> dict:
    splits = jax.random.split(jax.random.key(seed), 5)
    return {
        "tokens": gaussian(splits[0], (TOKENS, D), 1.0, 6.0, ((0, 8), (1, 64))),
        "up_weight": gaussian(splits[1], (D, FF), D ** -0.5, 0.078125, ((0, 64), (1, 8))),
        "down_weight": gaussian(splits[2], (FF, D), FF ** -0.5, 0.0390625, ((0, 8), (1, 64))),
        "grad_output": gaussian(splits[3], (TOKENS, D), 1.0, 6.0, ((0, 8), (1, 64))),
    }


root_scale = math.sqrt(2.0 / math.pi)
cubic_term = 0.044715

def gelu_value(hidden):
    curved = jnp.tanh(root_scale * (hidden + cubic_term * hidden * hidden * hidden))
    return 0.5 * hidden * (1.0 + curved)

def gelu_slope(hidden):
    curved = jnp.tanh(root_scale * (hidden + cubic_term * hidden * hidden * hidden))
    return 0.5 * (1.0 + curved) + 0.5 * hidden * (1.0 - curved * curved) * root_scale * (1.0 + 3.0 * cubic_term * hidden * hidden)

def rounded(summand):
    return lax.optimization_barrier(summand.astype(jnp.bfloat16)).astype(jnp.float32)

def contract_blocks(left_side, right_side, pieces):
    stride = left_side.shape[1] // pieces
    summed = jnp.zeros((left_side.shape[0], right_side.shape[1]), jnp.float32)
    for number in range(pieces):
        piece_sum = jnp.dot(left_side[:, number * stride:(number + 1) * stride], right_side[number * stride:(number + 1) * stride, :], preferred_element_type=jnp.float32)
        summed = summed + rounded(piece_sum)
    return summed

def reference(tokens, up_weight, down_weight, grad_output):
    hidden = contract_blocks(tokens, up_weight, N_GZ)
    activated = gelu_value(hidden).astype(jnp.bfloat16)
    output = contract_blocks(activated, down_weight, N_GX).astype(jnp.bfloat16)
    grad_act = contract_blocks(grad_output, down_weight.T, N_GZ)
    grad_hidden = (grad_act * gelu_slope(hidden)).astype(jnp.bfloat16)
    grad_tokens = contract_blocks(grad_hidden, up_weight.T, N_GX).astype(jnp.bfloat16)
    return (output, grad_tokens)
```

```python
import math

import jax
import jax.numpy as jnp
from jax import lax
from jax.sharding import Mesh
from jax.sharding import PartitionSpec as P

root_scale = math.sqrt(2.0 / math.pi)
cubic_term = 0.044715
SWAP = [(0, 1), (1, 0)]
AXES = ("zh", "y", "x", "core", "z4", "z2", "z1")


def gelu_value(hidden):
    curved = jnp.tanh(root_scale * (hidden + cubic_term * hidden * hidden * hidden))
    return 0.5 * hidden * (1.0 + curved)


def gelu_slope(hidden):
    curved = jnp.tanh(root_scale * (hidden + cubic_term * hidden * hidden * hidden))
    return 0.5 * (1.0 + curved) + 0.5 * hidden * (1.0 - curved * curved) * root_scale * (
        1.0 + 3.0 * cubic_term * hidden * hidden
    )


def swap(array, axis):
    return lax.ppermute(array, axis, SWAP)


def swap_blocks(array, bit, axis):
    return jnp.where(bit == 1, jnp.flip(array, axis), array)


def own_order(columns):
    rows = columns.shape[0]
    blocks = columns.reshape(rows, 2, 2, 2, 32)
    for axis, name in ((1, "z1"), (2, "z2"), (3, "z4")):
        blocks = swap_blocks(blocks, lax.axis_index(name), axis)
    return blocks.reshape(rows, 256)


def scatter_sum(partial_value):
    total = partial_value
    for name in ("z1", "z2", "z4"):
        half = total.shape[0] // 2
        sent = total[half:].astype(jnp.bfloat16)
        total = total[:half].astype(jnp.bfloat16).astype(jnp.float32) + swap(sent, name).astype(jnp.float32)
    return total


def gather_tokens(rows):
    for name in ("z4", "z2", "z1"):
        rows = jnp.concatenate([rows, swap(rows, name)], 0)
    return rows


def rows_of(shards):
    both = jnp.stack([shards, swap(shards, "zh")])
    all_y = lax.all_gather(both.reshape(384, 256), "y", axis=0, tiled=True)
    all_y = all_y.reshape(4, 2, 2, 96, 256).transpose(2, 1, 0, 3, 4)
    all_y = swap_blocks(all_y, lax.axis_index("zh"), 1).reshape(2, 768, 256)
    return all_y[0], all_y[1]


def finish(partial_value):
    blocks = partial_value.astype(jnp.bfloat16).reshape(2, 4, 96, 256)
    blocks = swap_blocks(blocks, lax.axis_index("zh"), 0).transpose(1, 0, 2, 3)
    parts = lax.all_to_all(blocks, "y", 0, 0, tiled=True)
    total = parts.astype(jnp.float32).sum(0)
    other = swap(total[1].astype(jnp.bfloat16), "zh")
    return (total[0] + other.astype(jnp.float32)).astype(jnp.bfloat16)


def contract(left, right, dims):
    return lax.dot_general(left, right, (dims, ((), ())), preferred_element_type=jnp.float32)


def local(tokens, up_weight, down_weight, grad_output):
    shards = own_order(jnp.concatenate([tokens.T, grad_output.T], 0))
    up_block = lax.all_gather(up_weight, ("x", "core"), axis=0, tiled=True)
    down_block = lax.all_gather(down_weight.T, ("x", "core"), axis=0, tiled=True)
    rows_in, grads_in = rows_of(shards)
    hidden = scatter_sum(contract(rows_in, up_block, ((0,), (0,))))
    activated = gather_tokens(gelu_value(hidden).astype(jnp.bfloat16))
    output = finish(contract(down_block, activated, ((1,), (1,))))
    grad_act = scatter_sum(contract(grads_in, down_block, ((0,), (0,))))
    grad_hidden = gather_tokens((grad_act * gelu_slope(hidden)).astype(jnp.bfloat16))
    grad_tokens = finish(contract(up_block, grad_hidden, ((1,), (1,))))
    return (own_order(output).T, own_order(grad_tokens).T)


def solution(mesh):
    fine = Mesh(mesh.devices.reshape(2, 4, 4, 2, 2, 2, 2), AXES)
    gx, gy, gz = ("zh", "y"), ("x", "core"), ("z4", "z2", "z1")
    in_specs = (P(gy, gz + gx), P(gz + gy, gx), P(gx, gz + gy), P(gy, gz + gx))
    out_specs = (P(gy, gz + gx), P(gy, gz + gx))
    return jax.shard_map(local, mesh=fine, in_specs=in_specs, out_specs=out_specs, check_vma=False)
```

```python
import math

import jax
import jax.numpy as jnp
from jax import lax
from jax.sharding import Mesh
from jax.sharding import PartitionSpec as P

root_scale = math.sqrt(2.0 / math.pi)
cubic_term = 0.044715
SWAP = [(0, 1), (1, 0)]
AXES = ("zh", "y", "x", "core", "z4", "z2", "z1")


def gelu_value(hidden):
    curved = jnp.tanh(root_scale * (hidden + cubic_term * hidden * hidden * hidden))
    return 0.5 * hidden * (1.0 + curved)


def gelu_slope(hidden):
    curved = jnp.tanh(root_scale * (hidden + cubic_term * hidden * hidden * hidden))
    return 0.5 * (1.0 + curved) + 0.5 * hidden * (1.0 - curved * curved) * root_scale * (
        1.0 + 3.0 * cubic_term * hidden * hidden
    )


def swap(array, axis):
    return lax.ppermute(array, axis, SWAP)


def flip_if(array, bit, axis):
    return jnp.where(bit == 1, jnp.flip(array, axis), array)


def half_swapped(weights):
    low, high = weights[:, :, :1536], weights[:, :, 1536:]
    bit = lax.axis_index("z1") == 1
    kept, sent = jnp.where(bit, high, low), jnp.where(bit, low, high)
    return jnp.stack([kept, swap(sent, "z1")], 1)


def neighbours(block):
    return tuple(lax.ppermute(block, "x", [(i, i ^ k) for i in range(4)]) for k in (1, 3))


def over_x(block, one, three):
    carried = jnp.where(lax.axis_index("core") == 0, one, three)
    onward = [(i, i ^ (6 if i % 2 == 0 else 2)) for i in range(8)]
    two = lax.ppermute(carried, ("x", "core"), onward)
    return [jnp.concatenate([p[i].reshape(192, -1) for p in (block, one, two, three)], 0) for i in (0, 1)]


def own_order(columns):
    blocks = columns.reshape(columns.shape[:-1] + (2, 2, 64))
    axis = blocks.ndim - 3
    blocks = flip_if(blocks, lax.axis_index("z2"), axis)
    blocks = flip_if(blocks, lax.axis_index("z4"), axis + 1)
    return blocks.reshape(columns.shape)


def over_zh(shards):
    return jnp.stack([shards, swap(shards, "zh")])


def gathered_rows(both):
    sent = jnp.broadcast_to(both[None], (8, 2, 192, 256))
    rows = lax.all_to_all(sent, ("y", "z1"), 0, 0, tiled=True)
    rows = rows.reshape(4, 2, 2, 2, 96, 256).transpose(3, 2, 0, 1, 4, 5)
    rows = flip_if(rows, lax.axis_index("zh"), 1)
    return flip_if(rows, lax.axis_index("z1"), 3)


def core_x_order(blocks):
    x = lax.axis_index("x")
    blocks = flip_if(blocks, x // 2, 0)
    blocks = flip_if(blocks, x % 2, 1)
    return flip_if(blocks, lax.axis_index("core"), 2)


def spread_sum(partial_value):
    total = partial_value
    for name in ("z2", "z4"):
        half = total.shape[0] // 2
        sent = total[half:].astype(jnp.bfloat16)
        total = total[:half].astype(jnp.bfloat16).astype(jnp.float32) + swap(sent, name).astype(jnp.float32)
    return total


def all_tokens(rows):
    for name in ("z4", "z2"):
        rows = jnp.concatenate([rows, swap(rows, name)], 0)
    return rows


def over_y(blocks):
    blocks = flip_if(blocks, lax.axis_index("zh"), 1)
    blocks = flip_if(blocks, lax.axis_index("z1"), 3)
    sent = blocks.transpose(2, 3, 0, 1, 4, 5).reshape(8, 2, 2, 96, 256)
    parts = lax.all_to_all(sent, ("y", "z1"), 0, 0, tiled=True)
    return parts.astype(jnp.float32).sum(0)


def contract(left, right, dims):
    return lax.dot_general(left, right, (dims, ((), ())), preferred_element_type=jnp.float32)


def product(rows, own, other):
    return contract(rows[0], own, ((0,), (0,))) + contract(rows[1], other, ((0,), (0,)))


def back_product(own, other, hidden):
    blocks = jnp.stack([contract(own, hidden, ((1,), (1,))), contract(other, hidden, ((1,), (1,)))])
    blocks = blocks.astype(jnp.bfloat16).reshape(2, 2, 2, 192, 256).transpose(1, 2, 0, 3, 4)
    return core_x_order(blocks).reshape(2, 4, 2, 96, 256)


def local(tokens, up_weight, down_weight, grad_output):
    shards = own_order(jnp.concatenate([tokens.T, grad_output.T], 0))
    halves = half_swapped(jnp.stack([up_weight, down_weight.T]))
    shards, halves = lax.optimization_barrier((shards, halves))
    both = over_zh(shards)
    one, three = neighbours(halves)
    both, one, three = lax.optimization_barrier((both, one, three))
    rows = gathered_rows(both)
    up_own, down_own = over_x(halves, one, three)
    up_other, down_other = swap(up_own, "core"), swap(down_own, "core")
    rows = core_x_order(rows.reshape(2, 2, 2, 2, 192, 256).transpose(1, 2, 3, 0, 4, 5))
    rows = rows.transpose(3, 2, 0, 1, 4, 5).reshape(2, 2, 768, 256)
    hidden = spread_sum(product(rows[0], up_own, up_other))
    activated = all_tokens(gelu_value(hidden).astype(jnp.bfloat16))
    grad_act = spread_sum(product(rows[1], down_own, down_other))
    grad_hidden = all_tokens((grad_act * gelu_slope(hidden)).astype(jnp.bfloat16))
    output = back_product(down_own, down_other, activated)
    grad_tokens = back_product(up_own, up_other, grad_hidden)
    sums = over_y(jnp.stack([output, grad_tokens]))
    other = swap(sums[:, 1].astype(jnp.bfloat16), "zh")
    both = own_order((sums[:, 0] + other.astype(jnp.float32)).astype(jnp.bfloat16))
    return (both[0].T, both[1].T)


def solution(mesh):
    fine = Mesh(mesh.devices.reshape(2, 4, 4, 2, 2, 2, 2), AXES)
    gx, gy, gz = ("zh", "y"), ("x", "core"), ("z4", "z2", "z1")
    in_specs = (P(gy, gz + gx), P(gz + gy, gx), P(gx, gz + gy), P(gy, gz + gx))
    out_specs = (P(gy, gz + gx), P(gy, gz + gx))
    return jax.shard_map(local, mesh=fine, in_specs=in_specs, out_specs=out_specs, check_vma=False)
```

```python
import math

import jax
import jax.numpy as jnp
from jax import lax
from jax.sharding import Mesh
from jax.sharding import PartitionSpec as P

root_scale = math.sqrt(2.0 / math.pi)
cubic_term = 0.044715
SWAP = [(0, 1), (1, 0)]
AXES = ("zh", "y", "x", "core", "z4", "z2", "z1")


def gelu_value(hidden):
    curved = jnp.tanh(root_scale * (hidden + cubic_term * hidden * hidden * hidden))
    return 0.5 * hidden * (1.0 + curved)


def gelu_slope(hidden):
    curved = jnp.tanh(root_scale * (hidden + cubic_term * hidden * hidden * hidden))
    return 0.5 * (1.0 + curved) + 0.5 * hidden * (1.0 - curved * curved) * root_scale * (
        1.0 + 3.0 * cubic_term * hidden * hidden
    )


def swap(array, axis):
    return lax.ppermute(array, axis, SWAP)


def flip_if(array, bit, axis):
    return jnp.where(bit == 1, jnp.flip(array, axis), array)


def half_swapped(weight):
    low, high = weight[:, :1536], weight[:, 1536:]
    bit = lax.axis_index("z4") == 1
    kept, sent = jnp.where(bit, high, low), jnp.where(bit, low, high)
    return jnp.concatenate([kept, swap(sent, "z4")], 0)


def neighbours(block):
    return tuple(lax.ppermute(block, "x", [(i, i ^ k) for i in range(4)]) for k in (1, 3))


def over_x(block, one, three):
    carried = jnp.where(lax.axis_index("core") == 0, one, three)
    onward = [(i, i ^ (6 if i % 2 == 0 else 2)) for i in range(8)]
    two = lax.ppermute(carried, ("x", "core"), onward)
    return jnp.concatenate([block, one, two, three], 0)


def own_order(columns):
    blocks = columns.reshape(columns.shape[:-1] + (2, 2, 64))
    axis = blocks.ndim - 3
    blocks = flip_if(blocks, lax.axis_index("z1"), axis)
    blocks = flip_if(blocks, lax.axis_index("z2"), axis + 1)
    return blocks.reshape(columns.shape)


def over_zh(shards):
    return jnp.stack([shards, swap(shards, "zh")])


def with_partner(both):
    return jnp.stack([both, swap(both, "z4")])


def gathered_rows(quad):
    sent = jnp.broadcast_to(quad.reshape(1, 768, 256), (4, 768, 256)).reshape(3072, 256)
    rows = lax.all_to_all(sent, "y", 0, 0, tiled=True)
    rows = rows.reshape(4, 2, 2, 2, 96, 256).transpose(3, 2, 0, 1, 4, 5)
    return flip_if(rows, lax.axis_index("zh"), 1)


def core_x_order(blocks):
    x = lax.axis_index("x")
    blocks = flip_if(blocks, x // 2, 0)
    blocks = flip_if(blocks, x % 2, 1)
    return flip_if(blocks, lax.axis_index("core"), 2)


def spread_sum(partial_value):
    total = partial_value
    for name in ("z1", "z2"):
        half = total.shape[0] // 2
        sent = total[half:].astype(jnp.bfloat16)
        total = total[:half].astype(jnp.bfloat16).astype(jnp.float32) + swap(sent, name).astype(jnp.float32)
    return total


def all_tokens(rows):
    for name in ("z2", "z1"):
        rows = jnp.concatenate([rows, swap(rows, name)], 0)
    return rows


def over_gx(blocks):
    blocks = flip_if(blocks, lax.axis_index("zh"), 1)
    sent = blocks.transpose(2, 3, 1, 0, 4, 5).reshape(3072, 256)
    parts = lax.all_to_all(sent, "y", 0, 0, tiled=True)
    total = parts.reshape(4, 2, 2, 2, 96, 256).astype(jnp.float32).sum(0)
    total = total[0] + swap(total[1].astype(jnp.bfloat16), "z4").astype(jnp.float32)
    total = total[0] + swap(total[1].astype(jnp.bfloat16), "zh").astype(jnp.float32)
    return total.astype(jnp.bfloat16)


def contract(left, right, dims):
    return lax.dot_general(left, right, (dims, ((), ())), preferred_element_type=jnp.float32)


def product(rows, own, other):
    return contract(rows[0], own, ((0,), (0,))) + contract(rows[1], other, ((0,), (0,)))


def back_product(own, other, hidden):
    blocks = jnp.stack([contract(own, hidden, ((1,), (1,))), contract(other, hidden, ((1,), (1,)))])
    blocks = blocks.astype(jnp.bfloat16).reshape(2, 2, 2, 192, 256).transpose(1, 2, 0, 3, 4)
    return core_x_order(blocks).reshape(2, 4, 2, 96, 256)


def local(tokens, up_weight, down_weight, grad_output):
    shards = own_order(jnp.concatenate([tokens.T, grad_output.T], 0))
    up_half, down_half = half_swapped(up_weight), half_swapped(down_weight.T)
    quad = with_partner(over_zh(shards))
    quad, up_half, down_half = lax.optimization_barrier((quad, up_half, down_half))
    near = neighbours(up_half) + neighbours(down_half)
    rows = gathered_rows(quad)
    up_own, down_own = over_x(up_half, *near[:2]), over_x(down_half, *near[2:])
    up_other, down_other = swap(up_own, "core"), swap(down_own, "core")
    rows = core_x_order(rows.reshape(2, 2, 2, 2, 192, 256).transpose(1, 2, 3, 0, 4, 5))
    rows = rows.transpose(3, 2, 0, 1, 4, 5).reshape(2, 2, 768, 256)
    hidden = spread_sum(product(rows[0], up_own, up_other))
    activated = all_tokens(gelu_value(hidden).astype(jnp.bfloat16))
    grad_act = spread_sum(product(rows[1], down_own, down_other))
    grad_hidden = all_tokens((grad_act * gelu_slope(hidden)).astype(jnp.bfloat16))
    output = back_product(down_own, down_other, activated)
    grad_tokens = back_product(up_own, up_other, grad_hidden)
    both = own_order(over_gx(jnp.stack([output, grad_tokens])))
    return (both[0].T, both[1].T)


def solution(mesh):
    fine = Mesh(mesh.devices.reshape(2, 4, 4, 2, 2, 2, 2), AXES)
    gx, gy, gz = ("zh", "y"), ("x", "core"), ("z4", "z2", "z1")
    in_specs = (P(gy, gz + gx), P(gz + gy, gx), P(gx, gz + gy), P(gy, gz + gx))
    out_specs = (P(gy, gz + gx), P(gy, gz + gx))
    return jax.shard_map(local, mesh=fine, in_specs=in_specs, out_specs=out_specs, check_vma=False)
```

```python
import math

import jax
import jax.numpy as jnp
from jax import lax
from jax.sharding import Mesh
from jax.sharding import PartitionSpec as P

root_scale = math.sqrt(2.0 / math.pi)
cubic_term = 0.044715
SWAP = [(0, 1), (1, 0)]
AXES = ("zh", "y", "x", "core", "z4", "z2", "z1")


def gelu_value(hidden):
    curved = jnp.tanh(root_scale * (hidden + cubic_term * hidden * hidden * hidden))
    return 0.5 * hidden * (1.0 + curved)


def gelu_slope(hidden):
    curved = jnp.tanh(root_scale * (hidden + cubic_term * hidden * hidden * hidden))
    return 0.5 * (1.0 + curved) + 0.5 * hidden * (1.0 - curved * curved) * root_scale * (
        1.0 + 3.0 * cubic_term * hidden * hidden
    )


def swap(array, axis):
    return lax.ppermute(array, axis, SWAP)


def flip_if(array, bit, axis):
    return jnp.where(bit == 1, jnp.flip(array, axis), array)


def half_swapped(weights):
    low, high = weights[:, :, :1536], weights[:, :, 1536:]
    bit = lax.axis_index("z2") == 1
    kept, sent = jnp.where(bit, high, low), jnp.where(bit, low, high)
    return jnp.stack([kept, swap(sent, "z2")], 1)


def neighbours(block):
    return tuple(lax.ppermute(block, "x", [(i, i ^ k) for i in range(4)]) for k in (1, 3))


def over_x(block, one, three):
    carried = jnp.where(lax.axis_index("core") == 0, one, three)
    onward = [(i, i ^ (6 if i % 2 == 0 else 2)) for i in range(8)]
    two = lax.ppermute(carried, ("x", "core"), onward)
    return [jnp.concatenate([p[i].reshape(192, -1) for p in (block, one, two, three)], 0) for i in (0, 1)]


def own_order(columns):
    blocks = columns.reshape(columns.shape[:-1] + (2, 2, 64))
    axis = blocks.ndim - 3
    blocks = flip_if(blocks, lax.axis_index("z1"), axis)
    blocks = flip_if(blocks, lax.axis_index("z4"), axis + 1)
    return blocks.reshape(columns.shape)


def gathered_rows(both):
    quad = jnp.concatenate([both, swap(both, "z2")], 0)
    sent = jnp.broadcast_to(quad[None], (4, 768, 256)).reshape(3072, 256)
    rows = lax.all_to_all(sent, "y", 0, 0, tiled=True)
    rows = rows.reshape(4, 2, 2, 2, 96, 256).transpose(3, 2, 0, 1, 4, 5)
    return flip_if(rows, lax.axis_index("zh"), 1)


def core_x_order(blocks):
    x = lax.axis_index("x")
    blocks = flip_if(blocks, x // 2, 0)
    blocks = flip_if(blocks, x % 2, 1)
    return flip_if(blocks, lax.axis_index("core"), 2)


def spread_sum(partial_value):
    total = partial_value
    for name in ("z1", "z4"):
        half = total.shape[0] // 2
        sent = total[half:].astype(jnp.bfloat16)
        total = total[:half].astype(jnp.bfloat16).astype(jnp.float32) + swap(sent, name).astype(jnp.float32)
    return total


def all_tokens(rows):
    for name in ("z4", "z1"):
        rows = jnp.concatenate([rows, swap(rows, name)], 0)
    return rows


def over_gx(blocks):
    blocks = flip_if(blocks, lax.axis_index("zh"), 1)
    sent = blocks.transpose(2, 3, 1, 0, 4, 5).reshape(3072, 256)
    parts = lax.all_to_all(sent, "y", 0, 0, tiled=True)
    total = parts.reshape(4, 2, 2, 2, 96, 256).astype(jnp.float32).sum(0)
    total = total[0] + swap(total[1].astype(jnp.bfloat16), "z2").astype(jnp.float32)
    total = total[0] + swap(total[1].astype(jnp.bfloat16), "zh").astype(jnp.float32)
    return total.astype(jnp.bfloat16)


def contract(left, right, dims):
    return lax.dot_general(left, right, (dims, ((), ())), preferred_element_type=jnp.float32)


def product(rows, own, other):
    return contract(rows[0], own, ((0,), (0,))) + contract(rows[1], other, ((0,), (0,)))


def back_product(own, other, hidden):
    blocks = jnp.stack([contract(own, hidden, ((1,), (1,))), contract(other, hidden, ((1,), (1,)))])
    blocks = blocks.astype(jnp.bfloat16).reshape(2, 2, 2, 192, 256).transpose(1, 2, 0, 3, 4)
    return core_x_order(blocks).reshape(2, 4, 2, 96, 256)


def local(tokens, up_weight, down_weight, grad_output):
    shards = own_order(jnp.concatenate([tokens.T, grad_output.T], 0))
    halves = half_swapped(jnp.stack([up_weight, down_weight.T]))
    shards, halves = lax.optimization_barrier((shards, halves))
    both = jnp.concatenate([shards, swap(shards, "zh")], 0)
    one, three = neighbours(halves)
    both, one, three = lax.optimization_barrier((both, one, three))
    rows = gathered_rows(both)
    up_own, down_own = over_x(halves, one, three)
    up_other, down_other = swap(up_own, "core"), swap(down_own, "core")
    rows = core_x_order(rows.reshape(2, 2, 2, 2, 192, 256).transpose(1, 2, 3, 0, 4, 5))
    rows = rows.transpose(3, 2, 0, 1, 4, 5).reshape(2, 2, 768, 256)
    hidden = spread_sum(product(rows[0], up_own, up_other))
    grad_act = spread_sum(product(rows[1], down_own, down_other))
    activated = all_tokens(gelu_value(hidden).astype(jnp.bfloat16))
    grad_hidden = all_tokens((grad_act * gelu_slope(hidden)).astype(jnp.bfloat16))
    output = back_product(down_own, down_other, activated)
    grad_tokens = back_product(up_own, up_other, grad_hidden)
    both = own_order(over_gx(jnp.stack([output, grad_tokens])))
    return (both[0].T, both[1].T)


def solution(mesh):
    fine = Mesh(mesh.devices.reshape(2, 4, 4, 2, 2, 2, 2), AXES)
    gx, gy, gz = ("zh", "y"), ("x", "core"), ("z4", "z2", "z1")
    in_specs = (P(gy, gz + gx), P(gz + gy, gx), P(gx, gz + gy), P(gy, gz + gx))
    out_specs = (P(gy, gz + gx), P(gy, gz + gx))
    return jax.shard_map(local, mesh=fine, in_specs=in_specs, out_specs=out_specs, check_vma=False)
```

```python
import math

import jax
import jax.numpy as jnp
from jax import lax
from jax.sharding import Mesh
from jax.sharding import PartitionSpec as P

root_scale = math.sqrt(2.0 / math.pi)
cubic_term = 0.044715
SWAP = [(0, 1), (1, 0)]
AXES = ("zh", "y", "x", "core", "z4", "z2", "z1")


def gelu_value(hidden):
    curved = jnp.tanh(root_scale * (hidden + cubic_term * hidden * hidden * hidden))
    return 0.5 * hidden * (1.0 + curved)


def gelu_slope(hidden):
    curved = jnp.tanh(root_scale * (hidden + cubic_term * hidden * hidden * hidden))
    return 0.5 * (1.0 + curved) + 0.5 * hidden * (1.0 - curved * curved) * root_scale * (
        1.0 + 3.0 * cubic_term * hidden * hidden
    )


def swap(array, axis):
    return lax.ppermute(array, axis, SWAP)


def flip_if(array, bit, axis):
    return jnp.where(bit == 1, jnp.flip(array, axis), array)


def half_swapped(weights):
    low, high = weights[:, :, :1536], weights[:, :, 1536:]
    bit = lax.axis_index("z2") == 1
    kept, sent = jnp.where(bit, high, low), jnp.where(bit, low, high)
    return jnp.stack([kept, swap(sent, "z2")], 1)


def neighbours(block):
    return tuple(lax.ppermute(block, "x", [(i, i ^ k) for i in range(4)]) for k in (1, 3))


def over_x(block, one, three):
    carried = jnp.where(lax.axis_index("core") == 0, one, three)
    onward = [(i, i ^ (6 if i % 2 == 0 else 2)) for i in range(8)]
    two = lax.ppermute(carried, ("x", "core"), onward)
    return [jnp.concatenate([p[i].reshape(192, -1) for p in (block, one, two, three)], 0) for i in (0, 1)]


def own_order(columns):
    blocks = columns.reshape(columns.shape[:-1] + (2, 2, 64))
    axis = blocks.ndim - 3
    blocks = flip_if(blocks, lax.axis_index("z1"), axis)
    blocks = flip_if(blocks, lax.axis_index("z4"), axis + 1)
    return blocks.reshape(columns.shape)


def gathered_rows(quad):
    sent = jnp.broadcast_to(quad[None], (4, 768, 256)).reshape(3072, 256)
    rows = lax.all_to_all(sent, "y", 0, 0, tiled=True)
    rows = rows.reshape(4, 2, 2, 2, 96, 256).transpose(3, 2, 0, 1, 4, 5)
    return flip_if(rows, lax.axis_index("zh"), 1)


def core_x_order(blocks):
    x = lax.axis_index("x")
    blocks = flip_if(blocks, x // 2, 0)
    blocks = flip_if(blocks, x % 2, 1)
    return flip_if(blocks, lax.axis_index("core"), 2)


def spread_sum(partial_value):
    total = partial_value
    for name in ("z1", "z4"):
        half = total.shape[0] // 2
        sent = total[half:].astype(jnp.bfloat16)
        total = total[:half].astype(jnp.bfloat16).astype(jnp.float32) + swap(sent, name).astype(jnp.float32)
    return total


def all_tokens(rows):
    for name in ("z4", "z1"):
        rows = jnp.concatenate([rows, swap(rows, name)], 0)
    return rows


def over_gx(blocks):
    blocks = flip_if(blocks, lax.axis_index("zh"), 1)
    sent = blocks.transpose(2, 3, 1, 0, 4, 5).reshape(3072, 256)
    parts = lax.all_to_all(sent, "y", 0, 0, tiled=True)
    total = parts.reshape(4, 2, 2, 2, 96, 256).astype(jnp.float32).sum(0)
    total = total[0] + swap(total[1].astype(jnp.bfloat16), "z2").astype(jnp.float32)
    total = total[0] + swap(total[1].astype(jnp.bfloat16), "zh").astype(jnp.float32)
    return total.astype(jnp.bfloat16)


def contract(left, right, dims):
    return lax.dot_general(left, right, (dims, ((), ())), preferred_element_type=jnp.float32)


def product(rows, own, other):
    return contract(rows[0], own, ((0,), (0,))) + contract(rows[1], other, ((0,), (0,)))


def back_product(own, other, hidden):
    blocks = jnp.stack([contract(own, hidden, ((1,), (1,))), contract(other, hidden, ((1,), (1,)))])
    blocks = blocks.astype(jnp.bfloat16).reshape(2, 2, 2, 192, 256).transpose(1, 2, 0, 3, 4)
    return core_x_order(blocks).reshape(2, 4, 2, 96, 256)


def local(tokens, up_weight, down_weight, grad_output):
    shards = own_order(jnp.concatenate([tokens.T, grad_output.T], 0))
    halves = half_swapped(jnp.stack([up_weight, down_weight.T]))
    both = jnp.concatenate([shards, swap(shards, "zh")], 0)
    quad = jnp.concatenate([both, swap(both, "z2")], 0)
    one, three = neighbours(halves)
    quad, one, three = lax.optimization_barrier((quad, one, three))
    rows = gathered_rows(quad)
    up_own, down_own = over_x(halves, one, three)
    up_other, down_other = swap(up_own, "core"), swap(down_own, "core")
    rows = core_x_order(rows.reshape(2, 2, 2, 2, 192, 256).transpose(1, 2, 3, 0, 4, 5))
    rows = rows.transpose(3, 2, 0, 1, 4, 5).reshape(2, 2, 768, 256)
    hidden = spread_sum(product(rows[0], up_own, up_other))
    grad_act = spread_sum(product(rows[1], down_own, down_other))
    activated = all_tokens(gelu_value(hidden).astype(jnp.bfloat16))
    grad_hidden = all_tokens((grad_act * gelu_slope(hidden)).astype(jnp.bfloat16))
    output = back_product(down_own, down_other, activated)
    grad_tokens = back_product(up_own, up_other, grad_hidden)
    both = own_order(over_gx(jnp.stack([output, grad_tokens])))
    return (both[0].T, both[1].T)


def solution(mesh):
    fine = Mesh(mesh.devices.reshape(2, 4, 4, 2, 2, 2, 2), AXES)
    gx, gy, gz = ("zh", "y"), ("x", "core"), ("z4", "z2", "z1")
    in_specs = (P(gy, gz + gx), P(gz + gy, gx), P(gx, gz + gy), P(gy, gz + gx))
    out_specs = (P(gy, gz + gx), P(gy, gz + gx))
    return jax.shard_map(local, mesh=fine, in_specs=in_specs, out_specs=out_specs, check_vma=False)
```
